512 devices in a mesh: dp: 32 (over z, x), mem: 16 (over y, core).
Axes of the slice: x: 4, y: 8, z: 8, core: 2. Of those that a mesh axis runs over, the one named last changes fastest.
Arguments:
- table: bfloat16 [2048, 4096], P(None, 'mem'), may hold values from -6 to 6
- block_ids: int32 [512, 4], P('dp'), may hold values from 0 to 15, all different within a row
- weights: bfloat16 [65536, 512], P(('dp', 'mem')), may hold values from -0.25 to 0.25
- grad_out: bfloat16 [65536, 4096], P(('dp', 'mem')), may hold values from -0.1796875 to 0.1796875
Outputs:
- values_out: bfloat16 [65536, 4096], P(('dp', 'mem'))
- grad_weights: bfloat16 [65536, 512], P(('dp', 'mem'))
- grad_table: bfloat16 [2048, 4096], P(None, 'mem')
The draws below stay inside these ranges and needn't reach their ends.
Inputs may be any that keep to these rules, and one draw needn't show every extreme that they name: `block_ids`: the 4 block ids of one tile are distinct.
All inputs are finite; a program needn't handle non-finite values.
Results may differ from the reference program's by a relative error of at most 0.001.
Values may be sent and summed in bfloat16 or wider, within the bound.
A program may use at most 64 MiB of HBM per device.

```python
import jax
import jax.numpy as jnp
from jax import lax

D = 4096
BLOCK = 128
SEL = 4
TILE = 128
BLOCKS = 16
TOKENS = 65536
TILES = 512
ROWS = 2048


def steps_of(key, dims, cuts, smallest, largest):
    factor_of, own = 1.0, jax.random.fold_in(key, 6)
    for dim, shards_of in cuts:
        steps = jnp.exp(jax.random.uniform(jax.random.fold_in(own, dim), (shards_of,), jnp.float32, smallest / len(cuts), largest / len(cuts)))
        factor_of = factor_of * jnp.repeat(steps, dims[dim] // shards_of).reshape([-1 if axis == dim else 1 for axis in range(len(dims))])
    return factor_of


def choose_distinct(key, rows, amount, top, lift):
    sequence = jax.random.permutation(jax.random.fold_in(key, 1), amount)
    boost = sequence
    for power in range(3):
        boost = boost * boost // amount
    boost = boost * lift // amount
    lots = jax.random.randint(jax.random.fold_in(key, 2), (rows, amount), 0, 4096) + boost
    sure = jax.random.permutation(jax.random.fold_in(key, 3), rows)[jnp.arange(amount) % rows]
    lots = jnp.where(jnp.arange(rows)[:, None] == sure[None, :], 1 << 14, lots)
    score = lots * amount + jnp.arange(amount)
    return lax.top_k(score.astype(jnp.int32), top)[1].astype(jnp.int32)


def noise(rng, extent, spread, most, cuts=(), kind=jnp.bfloat16):
    entries = spread * jax.random.normal(rng, extent, jnp.float32)
    if cuts:
        entries = entries * steps_of(rng, extent, cuts, -0.22, 0.18)
    return jnp.clip(entries, -most, most).astype(kind)


def setup_inputs(seed: int = 0) -> dict:
    arg_keys = jax.random.split(jax.random.key(seed), 5)
    table = noise(arg_keys[0], (ROWS, D), 1.0, 6.0, ((1, 16),))
    block_ids = choose_distinct(arg_keys[1], TILES, BLOCKS, SEL, 4096)
    weights = noise(arg_keys[2], (TOKENS, SEL * BLOCK), (SEL * BLOCK) ** -0.5, 0.25, ((0, 512),))
    grad_out = noise(arg_keys[3], (TOKENS, D), 0.03, 0.1796875, ((0, 512),))
    return {"table": table, "block_ids": block_ids, "weights": weights, "grad_out": grad_out}


def reference(table, block_ids, weights, grad_out):
    blocks = table.reshape(BLOCKS, BLOCK, D)
    tile_w = weights.reshape(TILES, TILE, SEL * BLOCK)
    tile_g = grad_out.reshape(TILES, TILE, D)

    def one_tile(carry, packed):
        ids, wt, gt = packed
        chosen = blocks[ids].reshape(SEL * BLOCK, D)
        out = jnp.dot(wt, chosen, preferred_element_type=jnp.float32).astype(jnp.bfloat16)
        gw = jnp.dot(gt, chosen.T, preferred_element_type=jnp.float32).astype(jnp.bfloat16)
        dsel = jnp.dot(wt.T, gt, preferred_element_type=jnp.float32).reshape(SEL, BLOCK, D)
        carry = carry.at[ids].add(dsel)
        return carry, (out, gw)

    init = jnp.zeros((BLOCKS, BLOCK, D), jnp.float32)
    total, (outs, gws) = lax.scan(one_tile, init, (block_ids, tile_w, tile_g))
    return (outs.reshape(TOKENS, D), gws.reshape(TOKENS, SEL * BLOCK),
            total.reshape(ROWS, D).astype(jnp.bfloat16))
```

```python
import functools

import jax
import jax.numpy as jnp
from jax import lax
from jax.experimental import pallas as pl
from jax.experimental.pallas import tpu as pltpu
from jax.sharding import PartitionSpec as P

MESH = pl.DeviceIdType.MESH
BLOCK = 128
SEL = 4
TILE = 128
HALF = 128
NX = 4


def kernel(
    nx, ny, nz, rows, width,
    ids_ref, idx_ref, table_ref, w_ref, g_ref,
    vout_ref, gw_ref, tout_ref,
    T, Wt, Gr, acc, ra, rb, r2a, r2b, O, V, GW,
    send, recv, local,
):
    dp, mem = lax.axis_index("dp"), lax.axis_index("mem")
    z, x = dp // nx, dp % nx
    y, c = mem // 2, mem % 2
    s = 1 - 2 * c
    n_mem = 2 * ny
    blocks = rows // BLOCK
    zero_slot = n_mem * SEL
    na = (ny - 1) // 2
    nb = ny - 1 - na
    xr, zr, sh = rows // nx, rows // nz, rows // (nx * nz)

    def dev(xx, yy, zz, cc):
        return (zz * nx + xx, yy * 2 + cc)

    sib = dev(x, y, z, 1 - c)

    def wrap(v, n):
        return (v + 4 * n) % n

    def row(start, size):
        return pl.ds(pl.multiple_of(start, size), size)

    def rows_of(ref, lead, start, size):
        if size >= BLOCK:
            return ref.at[(*lead, pl.ds(start // BLOCK, size // BLOCK))]
        return ref.at[(*lead, start // BLOCK, row(start % BLOCK, size))]

    everything = []

    def remote(src, dst, device):
        k = len(everything)
        copy = pltpu.make_async_remote_copy(
            src_ref=src, dst_ref=dst, send_sem=send.at[k], recv_sem=recv.at[k],
            device_id=device, device_id_type=MESH,
        )
        copy.start()
        everything.append(copy)
        return copy

    def next_x(d):
        return dev(wrap(x + d, nx), y, z, c)

    def next_y(d):
        return dev(x, wrap(y + d, ny), z, c)

    def next_z(d):
        return dev(x, y, wrap(z + d, nz), c)

    barrier = pltpu.get_barrier_semaphore()
    peers = [(dp, (mem + k) % n_mem) for k in range(1, n_mem)]
    peers += [next_x(k) for k in range(1, nx)] + [next_z(k) for k in range(1, nz)]
    for p in peers:
        pl.semaphore_signal(barrier, inc=1, device_id=p, device_id_type=MESH)
    pl.semaphore_wait(barrier, len(peers))

    share_a, share_b = z * zr + x * sh, x * xr + z * sh
    order = sorted(range(1, ny), key=lambda j: min(j, ny - j))
    shares = {}
    for j in order:
        at = share_a if j <= na else share_b
        shares[j] = remote(rows_of(table_ref, (), at, sh), rows_of(T, (j, c), at, sh), next_y(-j))
    own = pltpu.make_async_copy(table_ref, T.at[0, c], local.at[0])
    own.start()

    Wt[zero_slot] = jnp.zeros((BLOCK, TILE), jnp.bfloat16)
    for k in range(SEL):
        Wt[mem * SEL + k] = w_ref[:, k * BLOCK:(k + 1) * BLOCK].astype(jnp.float32).T.astype(jnp.bfloat16)

    def w_piece(d, back):
        return Wt.at[pl.ds((wrap(y - d * back, ny) * 2 + c) * SEL, SEL)]

    def w_hop(d, h):
        p = w_piece(d, h - 1)
        return remote(p, p, next_y(d))

    sib_w = []

    def w_sib(d, back):
        p = w_piece(d, back)
        sib_w.append(remote(p, p, sib))

    wl, ws = w_hop(s, 1), (w_hop(-s, 1) if ny > 2 else None)
    w_sib(s, 0)
    sib_t = [remote(table_ref, T.at[0, c], sib)]

    g_copies = []

    def g_send(ks):
        for k in ks:
            m = (mem + k) % n_mem
            g_copies.append(
                remote(g_ref.at[:, row(m * width, width)], Gr.at[mem], (dp, m))
            )

    g_order = list(range(1, n_mem))
    per = -(-len(g_order) // (ny // 2))
    g_batches = [g_order[i:i + per] for i in range(0, len(g_order), per)]
    g_own = pltpu.make_async_copy(g_ref.at[:, row(mem * width, width)], Gr.at[mem], local.at[1])
    g_own.start()

    def ax_hop(d, h):
        p = rows_of(T, (slice(1, 1 + na), c), z * zr + wrap(x - d * (h - 1), nx) * sh, sh)
        return remote(p, p, next_x(d))

    def az_piece(d, back):
        return rows_of(T, (slice(1, 1 + na), c), wrap(z - d * back, nz) * zr, zr)

    def az_hop(d, h):
        p = az_piece(d, h - 1)
        return remote(p, p, next_z(d))

    def bz_hop(d, h):
        p = rows_of(T, (slice(1 + na, ny), c), x * xr + wrap(z - d * (h - 1), nz) * sh, sh)
        return remote(p, p, next_z(d))

    def bx_piece(d, back):
        return rows_of(T, (slice(1 + na, ny), c), wrap(x - d * back, nx) * xr, xr)

    def bx_hop(d, h):
        p = bx_piece(d, h - 1)
        return remote(p, p, next_x(d))

    def t_sib(p):
        sib_t.append(remote(p, p, sib))

    lx, lz, ly = nx // 2, nz // 2, ny // 2

    for j in range(1, ny):
        if j <= na:
            shares[j].wait_recv()
    axl = ax_hop(s, 1)
    axs = ax_hop(-s, 1) if lx > 1 else None
    for j in range(1, ny):
        if j > na:
            shares[j].wait_recv()
    bzl = bz_hop(s, 1)
    bzs = bz_hop(-s, 1) if lz > 1 else None

    azl = azs = None
    for h in range(1, max(ly, lz, lx) + 1):
        if h <= len(g_batches):
            g_send(g_batches[h - 1])
        if h <= lx:
            axl.wait_recv()
            if h < lx:
                axl = ax_hop(s, h + 1)
            if h < lx:
                axs.wait_recv()
                if h < lx - 1:
                    axs = ax_hop(-s, h + 1)
            if h == lx:
                azl = az_hop(s, 1)
                azs = az_hop(-s, 1) if lz > 1 else None
                t_sib(az_piece(s, 0))
        if h <= lz:
            bzl.wait_recv()
            if h < lz:
                bzl = bz_hop(s, h + 1)
            if h < lz:
                bzs.wait_recv()
                if h < lz - 1:
                    bzs = bz_hop(-s, h + 1)
        if h <= ly:
            wl.wait_recv()
            if h < ly:
                wl = w_hop(s, h + 1)
            w_sib(s, h)
            if h < ly:
                ws.wait_recv()
                if h < ly - 1:
                    ws = w_hop(-s, h + 1)
                w_sib(-s, h)
    bxl = bx_hop(s, 1)
    bxs = bx_hop(-s, 1) if lx > 1 else None
    t_sib(bx_piece(s, 0))

    state = dict(azl=azl, azs=azs, bxl=bxl, bxs=bxs)

    def az_step(h):
        if h > lz:
            return
        state["azl"].wait_recv()
        if h < lz:
            state["azl"] = az_hop(s, h + 1)
        t_sib(az_piece(s, h))
        if h < lz:
            state["azs"].wait_recv()
            if h < lz - 1:
                state["azs"] = az_hop(-s, h + 1)
            t_sib(az_piece(-s, h))

    def bx_step(h):
        if h > lx:
            return
        state["bxl"].wait_recv()
        if h < lx:
            state["bxl"] = bx_hop(s, h + 1)
        t_sib(bx_piece(s, h))
        if h < lx:
            state["bxs"].wait_recv()
            if h < lx - 1:
                state["bxs"] = bx_hop(-s, h + 1)
            t_sib(bx_piece(-s, h))

    az_step(1)
    az_step(2)

    for g in g_copies:
        g.wait_recv()
    g_own.wait()
    for w in sib_w:
        w.wait_recv()

    def grad_rows(i, _):
        parts = []
        for b in range(2):
            parts.append(
                jnp.concatenate([Wt[idx_ref[2 * i + b, t]] for t in range(n_mem)], axis=1)
            )
        lhs = jnp.concatenate(parts, axis=0)
        rhs = Gr[...].reshape(n_mem * TILE, width)
        r = jnp.dot(lhs, rhs, preferred_element_type=jnp.float32)
        at = row(i * 2 * BLOCK, 2 * BLOCK)
        acc[0, at, :] = r[:, :HALF]
        acc[1, at, :] = r[:, HALF:]
        return 0

    lax.fori_loop(0, blocks // 2, grad_rows, 0)

    def chunk(half, start, size):
        return (half, row(start, size), slice(None))

    def a_send(d, hops, h, bufs):
        dest = wrap(x + d * (hops - h + 1), nx)
        own_part = chunk(0, dest * xr, xr)
        if h == 1:
            src = acc.at[own_part]
        else:
            bufs[h - 2][...] += acc[own_part]
            src = bufs[h - 2]
        return remote(src, bufs[h - 1], next_x(d))

    def b_send(d, hops, h, bufs):
        dest = wrap(z + d * (hops - h + 1), nz)
        own_part = chunk(1, dest * zr, zr)
        if h == 1:
            src = acc.at[own_part]
        else:
            bufs[h - 2][...] += acc[own_part]
            src = bufs[h - 2]
        return remote(src, bufs[h - 1], next_z(d))

    ra_l, ra_s = [ra.at[i] for i in range(lx)], [ra.at[lx + i] for i in range(lx - 1)]
    rb_l, rb_s = [rb.at[i] for i in range(lz)], [rb.at[lz + i] for i in range(lz - 1)]
    al = a_send(s, lx, 1, ra_l)
    as_ = a_send(-s, lx - 1, 1, ra_s) if lx > 1 else None
    bl = b_send(s, lz, 1, rb_l)
    bs = b_send(-s, lz - 1, 1, rb_s) if lz > 1 else None
    bx_step(1)
    second_a = []
    for h in range(1, max(lx, lz) + 1):
        if h <= lz:
            bl.wait_recv()
            if h < lz:
                bl = b_send(s, lz, h + 1, rb_l)
            if h < lz:
                bs.wait_recv()
                if h < lz - 1:
                    bs = b_send(-s, lz - 1, h + 1, rb_s)
        if h <= lx:
            al.wait_recv()
            if h < lx:
                al = a_send(s, lx, h + 1, ra_l)
            if h < lx:
                as_.wait_recv()
                if h < lx - 1:
                    as_ = a_send(-s, lx - 1, h + 1, ra_s)
        if h == lx:
            mine = chunk(0, x * xr, xr)
            total = acc[mine] + ra_l[-1][...]
            if lx > 1:
                total = total + ra_s[-1][...]
            acc[mine] = total
            for k in range(1, nz):
                src = acc.at[chunk(0, x * xr + wrap(z + k, nz) * sh, sh)]
                second_a.append(remote(src, r2a.at[k - 1], next_z(k)))
        if h == 1:
            az_step(3)
    mine = chunk(1, z * zr, zr)
    total = acc[mine] + rb_l[-1][...]
    if lz > 1:
        total = total + rb_s[-1][...]
    acc[mine] = total
    second_b = []
    for k in range(1, nx):
        src = acc.at[chunk(1, z * zr + wrap(x + k, nx) * sh, sh)]
        second_b.append(remote(src, r2b.at[k - 1], next_x(k)))

    for r in second_a:
        r.wait_recv()
    mine_a = chunk(0, x * xr + z * sh, sh)
    total = acc[mine_a]
    for k in range(nz - 1):
        total = total + r2a[k]
    O[mine_a] = total.astype(jnp.bfloat16)
    out_az = [remote(O.at[mine_a], O.at[mine_a], next_z(k)) for k in range(1, nz)]
    for r in second_b:
        r.wait_recv()
    mine_b = chunk(1, z * zr + x * sh, sh)
    total = acc[mine_b]
    for k in range(nx - 1):
        total = total + r2b[k]
    O[mine_b] = total.astype(jnp.bfloat16)
    out_bx = [remote(O.at[mine_b], O.at[mine_b], next_x(k)) for k in range(1, nx)]

    bx_step(2)
    az_step(4)

    for r in out_az:
        r.wait_recv()
    piece = O.at[chunk(0, x * xr, xr)]
    out_ax = [remote(piece, piece, next_x(k)) for k in range(1, nx)]
    for r in out_bx:
        r.wait_recv()

    def ob_hop(d, h):
        p = O.at[chunk(1, wrap(z - d * (h - 1), nz) * zr, zr)]
        return remote(p, p, next_z(d))

    obl = ob_hop(s, 1)
    obs = ob_hop(-s, 1) if lz > 1 else None

    own.wait()
    for t in sib_t:
        t.wait_recv()
    GW[...] = jnp.zeros_like(GW)
    def columns(i, _):
        j, cc = i // 2, i % 2
        at = row((((j + y) % ny) * 2 + cc) * width, width)
        sel = jnp.concatenate(
            [T[j, cc, ids_ref[mem, k]] for k in range(SEL)], axis=0
        )
        V[:, at] = jnp.dot(w_ref[...], sel, preferred_element_type=jnp.float32).astype(jnp.bfloat16)
        GW[...] += lax.dot_general(
            g_ref[:, at], sel, (((1,), (1,)), ((), ())), preferred_element_type=jnp.float32
        )
        return 0

    def some(lo, hi):
        lax.fori_loop(lo, hi, columns, 0)

    part = (n_mem + lz - 1) // lz
    for h in range(1, lz + 1):
        some(min((h - 1) * part, n_mem), min(h * part, n_mem))
        obl.wait_recv()
        if h < lz:
            obl = ob_hop(s, h + 1)
        if h < lz:
            obs.wait_recv()
            if h < lz - 1:
                obs = ob_hop(-s, h + 1)
    gw_ref[...] = GW[...].astype(jnp.bfloat16)
    v_out = pltpu.make_async_copy(V, vout_ref, local.at[2])
    v_out.start()
    for r in out_ax:
        r.wait_recv()
    t_outs = [
        pltpu.make_async_copy(O.at[h], tout_ref.at[:, h * HALF:(h + 1) * HALF], local.at[3 + h])
        for h in range(2)
    ]
    for t in t_outs:
        t.start()
    for r in everything:
        r.wait_send()
    v_out.wait()
    for t in t_outs:
        t.wait()


def shards(nx, ny, nz, table, block_ids, weights, grad_out):
    rows, width = table.shape
    n_mem = 2 * ny
    blocks = rows // BLOCK
    hit = block_ids[None, :, :] == jnp.arange(blocks, dtype=jnp.int32)[:, None, None]
    at = jnp.arange(n_mem, dtype=jnp.int32)[:, None] * SEL + jnp.arange(SEL, dtype=jnp.int32)[None, :]
    idx = jnp.min(jnp.where(hit, at[None], n_mem * SEL), axis=-1)
    xr, zr, sh = rows // nx, rows // nz, rows // (nx * nz)
    n_copies = 160
    vmem = pl.BlockSpec(memory_space=pltpu.VMEM)
    smem = pl.BlockSpec(memory_space=pltpu.SMEM)
    hbm = pl.BlockSpec(memory_space=pl.ANY)
    return pl.pallas_call(
        functools.partial(kernel, nx, ny, nz, rows, width),
        out_shape=(
            jax.ShapeDtypeStruct(grad_out.shape, jnp.bfloat16),
            jax.ShapeDtypeStruct(weights.shape, jnp.bfloat16),
            jax.ShapeDtypeStruct(table.shape, jnp.bfloat16),
        ),
        in_specs=[smem, smem, hbm, vmem, vmem],
        out_specs=(hbm, vmem, hbm),
        scratch_shapes=[
            pltpu.VMEM((ny, 2, blocks, BLOCK, width), jnp.bfloat16),
            pltpu.VMEM((n_mem * SEL + 1, BLOCK, TILE), jnp.bfloat16),
            pltpu.VMEM((n_mem, TILE, width), jnp.bfloat16),
            pltpu.VMEM((2, rows, HALF), jnp.float32),
            pltpu.VMEM((nx - 1, xr, HALF), jnp.float32),
            pltpu.VMEM((nz - 1, zr, HALF), jnp.float32),
            pltpu.VMEM((nz - 1, sh, HALF), jnp.float32),
            pltpu.VMEM((nx - 1, sh, HALF), jnp.float32),
            pltpu.VMEM((2, rows, HALF), jnp.bfloat16),
            pltpu.VMEM(grad_out.shape, jnp.bfloat16),
            pltpu.VMEM(weights.shape, jnp.float32),
            pltpu.SemaphoreType.DMA((n_copies,)),
            pltpu.SemaphoreType.DMA((n_copies,)),
            pltpu.SemaphoreType.DMA((5,)),
        ],
        compiler_params=pltpu.CompilerParams(
            collective_id=0, has_side_effects=True, vmem_limit_bytes=56 * 1024 * 1024
        ),
    )(block_ids, idx, table.reshape(blocks, BLOCK, width), weights, grad_out)


def solution(mesh):
    nx = NX
    nz = mesh.shape["dp"] // nx
    ny = mesh.shape["mem"] // 2
    return jax.shard_map(
        functools.partial(shards, nx, ny, nz),
        mesh=mesh,
        in_specs=(P(None, "mem"), P("dp", None), P(("dp", "mem"), None), P(("dp", "mem"), None)),
        out_specs=(P(("dp", "mem"), None), P(("dp", "mem"), None), P(None, "mem")),
        check_vma=False,
    )
```

```python
import functools

import jax
import jax.numpy as jnp
from jax import lax
from jax.experimental import pallas as pl
from jax.experimental.pallas import tpu as pltpu
from jax.sharding import PartitionSpec as P

MESH = pl.DeviceIdType.MESH
BLOCK = 128
SEL = 4
TILE = 128
HALF = 128
NX = 4
N_SEMS = 72


def kernel(
    nx, ny, nz, rows, width,
    ids_ref, idx_ref, table_ref, w_ref, g_ref,
    vout_ref, gw_ref, tout_ref,
    T, N, Wt, Gr, acc, rp1, rp2, rq1, rq2, O, V, GW,
    send, recv, local,
):
    dp, mem = lax.axis_index("dp"), lax.axis_index("mem")
    z, x = dp // nx, dp % nx
    y, c = mem // 2, mem % 2
    s = 1 - 2 * c
    n_mem = 2 * ny
    blocks = rows // BLOCK
    zero_slot = n_mem * SEL
    far = ny - 3
    na = 2 * far // 5
    xr, zr, sh = rows // nx, rows // nz, rows // (nx * nz)
    lx, lz, ly = nx // 2, nz // 2, ny // 2

    def dev(xx, yy, zz, cc):
        return (zz * nx + xx, yy * 2 + cc)

    sib = dev(x, y, z, 1 - c)

    def wrap(v, n):
        return (v + 4 * n) % n

    def row(start, size):
        return pl.ds(pl.multiple_of(start, size), size)

    def rows_of(ref, lead, start, size):
        if size >= BLOCK:
            return ref.at[(*lead, pl.ds(start // BLOCK, size // BLOCK))]
        return ref.at[(*lead, start // BLOCK, row(start % BLOCK, size))]

    def next_x(d):
        return dev(wrap(x + d, nx), y, z, c)

    def next_y(d):
        return dev(x, wrap(y + d, ny), z, c)

    def next_z(d):
        return dev(x, y, wrap(z + d, nz), c)

    used = [0]
    ends = []

    class Group:
        def __init__(self, out=None, into=None):
            self.k = used[0]
            used[0] += 1
            self.out, self.into = out, into
            ends.append(self)

        def start(self, src, dst, device):
            copy = pltpu.make_async_remote_copy(
                src_ref=src, dst_ref=dst, send_sem=send.at[self.k], recv_sem=recv.at[self.k],
                device_id=device, device_id_type=MESH,
            )
            copy.start()
            if self.out is None:
                self.out = src
            if self.into is None:
                self.into = dst
            return self

        def wait_recv(self):
            pltpu.make_async_copy(self.into, self.into, recv.at[self.k]).wait()

        def wait_send(self):
            pltpu.make_async_copy(self.out, self.out, send.at[self.k]).wait()

    def one(src, dst, device):
        return Group().start(src, dst, device)

    own = pltpu.make_async_copy(table_ref, T.at[0, c], local.at[0])
    own.start()
    g_own = [
        pltpu.make_async_copy(g_ref.at[:, row(mem * width + h * HALF, HALF)], Gr.at[h, mem], local.at[1 + h])
        for h in range(2)
    ]
    for g in g_own:
        g.start()
    barrier = pltpu.get_barrier_semaphore()
    peers = [(min(k // 2, ny - k // 2), (dp, (mem + k) % n_mem)) for k in range(1, n_mem)]
    peers += [(min(k, nx - k), next_x(k)) for k in range(1, nx)]
    peers += [(min(k, nz - k), next_z(k)) for k in range(1, nz)]
    peers = [p for _, p in sorted(peers, key=lambda p: -p[0])]
    for p in peers:
        pl.semaphore_signal(barrier, inc=1, device_id=p, device_id_type=MESH)
    Wt[zero_slot] = jnp.zeros((BLOCK, TILE), jnp.bfloat16)
    for k in range(SEL):
        Wt[mem * SEL + k] = w_ref[:, k * BLOCK:(k + 1) * BLOCK].astype(jnp.float32).T.astype(jnp.bfloat16)
    pl.semaphore_wait(barrier, len(peers))

    share_a, share_b = z * zr + x * sh, x * xr + z * sh
    a_planes, b_planes = slice(1, 1 + na), slice(1 + na, 1 + far)
    in_a = rows_of(T, (a_planes, c), share_a, sh)
    in_b = rows_of(T, (b_planes, c), share_b, sh)
    shares_a, shares_b = Group(in_a, in_a), Group(in_b, in_b)
    for i in sorted(range(1, 1 + far), key=lambda i: min(i + 1, ny - i - 1)):
        group, at = (shares_a, share_a) if i <= na else (shares_b, share_b)
        group.start(rows_of(table_ref, (), at, sh), rows_of(T, (i, c), at, sh), next_y(-(i + 1)))

    def w_piece(d, back):
        return Wt.at[pl.ds((wrap(y - d * back, ny) * 2 + c) * SEL, SEL)]

    def w_hop(d, h):
        p = w_piece(d, h - 1)
        return one(p, p, next_y(d))

    all_w = Wt.at[0:ny * SEL]
    sib_w = Group(all_w, all_w)

    def w_sib(d, back):
        p = w_piece(d, back)
        sib_w.start(p, p, sib)

    wl, ws = w_hop(s, 1), w_hop(-s, 1)
    w_sib(s, 0)
    sib_t = Group(T.at[:, c], T.at[:, 1 - c])
    sib_t.start(table_ref, T.at[0, c], sib)

    def t_sib(p):
        sib_t.start(p, p, sib)

    def g_send(h):
        others = Gr.at[h, 0:n_mem - 1]
        group = Group(others, others)
        for k in sorted(range(1, n_mem), key=lambda k: min(k // 2, ny - k // 2)):
            m = (mem + k) % n_mem
            group.start(g_ref.at[:, row(m * width + h * HALF, HALF)], Gr.at[h, mem], (dp, m))
        return group

    g1 = g_send(0)

    def ax_piece(back):
        return rows_of(T, (a_planes, c), z * zr + wrap(x - back, nx) * sh, sh)

    def az_piece(i, d, back):
        return rows_of(T, (i, c), wrap(z - d * back, nz) * zr, zr)

    def az_chunk(d, back):
        return rows_of(T, (a_planes, c), wrap(z - d * back, nz) * zr, zr)

    def b_piece(dx, xback, dz, zback):
        return rows_of(T, (b_planes, c), wrap(x - dx * xback, nx) * xr + wrap(z - dz * zback, nz) * sh, sh)

    def bx_chunk(d, back):
        return rows_of(T, (b_planes, c), wrap(x - d * back, nx) * xr, xr)

    def bz_hop(d, h):
        p = b_piece(s, 0, d, h - 1)
        return one(p, p, next_z(d))

    bx_short = Group(bx_chunk(-s, 0), bx_chunk(-s, 1))
    bx_last = Group(bx_chunk(s, 1), bx_chunk(s, 2))
    bx_first = {}

    def bx_start(d, back):
        p = b_piece(s, 0, d, back)
        bx_first[(d is s, back)] = one(p, p, next_x(s))
        bx_short.start(p, p, next_x(-s))

    def bx_forward(d, back):
        bx_first[(d is s, back)].wait_recv()
        p = b_piece(s, 1, d, back)
        bx_last.start(p, p, next_x(s))

    minus = -s
    shares_a.wait_recv()
    others = T.at[a_planes, c, 0, pl.ds(0, (nx - 1) * sh)] if (nx - 1) * sh <= BLOCK else None
    ax = []
    for k in range(1, nx):
        p = ax_piece(0)
        ax.append(one(p, p, next_x(k)))
    shares_b.wait_recv()
    bzl, bzs = bz_hop(s, 1), bz_hop(minus, 1) if lz > 1 else None
    bx_start(s, 0)

    azl, azs = {}, {}

    def az_step(h):
        if h > lz:
            return
        for i in range(1, 1 + na):
            if h > 0:
                azl[i].wait_recv()
            if h < lz:
                p = az_piece(i, s, h)
                azl[i] = one(p, p, next_z(s))
            if 0 < h < lz:
                azs[i].wait_recv()
            if h < lz - 1:
                p = az_piece(i, minus, h)
                azs[i] = one(p, p, next_z(minus))
        t_sib(az_chunk(s, h))
        if 0 < h < lz:
            t_sib(az_chunk(minus, h))

    def w_step(h):
        nonlocal wl, ws
        if h > ly:
            return
        wl.wait_recv()
        if h < ly:
            wl = w_hop(s, h + 1)
        w_sib(s, h)
        if h < ly:
            ws.wait_recv()
            if h < ly - 1:
                ws = w_hop(minus, h + 1)
            w_sib(minus, h)

    def bz_step(h):
        nonlocal bzl, bzs
        if h > lz:
            return
        bzl.wait_recv()
        if h < lz:
            bzl = bz_hop(s, h + 1)
        bx_start(s, h)
        if h < lz:
            bzs.wait_recv()
            if h < lz - 1:
                bzs = bz_hop(minus, h + 1)
            bx_start(minus, h)

    def bx_step(h):
        if h > lz:
            return
        bx_forward(s, h)
        if 0 < h < lz:
            bx_forward(minus, h)

    w_step(1)
    bz_step(1)
    for r in ax:
        r.wait_recv()
    az_step(0)
    w_step(2)
    bz_step(2)
    bx_step(0)
    w_step(3)
    g2 = g_send(1)
    az_step(1)
    bz_step(3)
    bx_step(1)
    w_step(4)
    bz_step(4)
    t_sib(bx_chunk(s, 0))
    az_step(2)
    bx_step(2)

    def grad(h):
        def grad_rows(i, _):
            parts = []
            for b in range(2):
                parts.append(
                    jnp.concatenate([Wt[idx_ref[2 * i + b, t]] for t in range(n_mem)], axis=1)
                )
            lhs = jnp.concatenate(parts, axis=0)
            rhs = Gr[h].reshape(n_mem * TILE, HALF)
            r = jnp.dot(lhs, rhs, preferred_element_type=jnp.float32)
            acc[h, row(i * 2 * BLOCK, 2 * BLOCK), :] = r
            return 0

        lax.fori_loop(0, blocks // 2, grad_rows, 0)

    top = rows // 2
    px, pz = top // nx, top // (nx * nz)
    qz, qx = top // nz, top // (nx * nz)

    def reduction(h):
        def at(ref, start, size):
            return ref.at[h, row(start, size), :]

        def bytes_of(ref, size):
            return ref.at[h, 0:size, :]

        def p1():
            group = Group(rp1.at[h], rp1.at[h])
            for k in range(1, nx):
                group.start(at(acc, wrap(x + k, nx) * px, px), rp1.at[h, k - 1], next_x(k))
            return group

        def q1():
            group = Group(rq1.at[h], rq1.at[h])
            for k in range(1, nz):
                group.start(at(acc, top + wrap(z + k, nz) * qz, qz), rq1.at[h, k - 1], next_z(k))
            return group

        def p2():
            mine = row(x * px, px)
            total = acc[h, mine, :]
            for k in range(nx - 1):
                total = total + rp1[h, k]
            acc[h, mine, :] = total
            group = Group(rp2.at[h], rp2.at[h])
            for k in range(1, nz):
                group.start(at(acc, x * px + wrap(z + k, nz) * pz, pz), rp2.at[h, k - 1], next_z(k))
            return group

        def q2():
            mine = row(top + z * qz, qz)
            total = acc[h, mine, :]
            for k in range(nz - 1):
                total = total + rq1[h, k]
            acc[h, mine, :] = total
            group = Group(rq2.at[h], rq2.at[h])
            for k in range(1, nx):
                group.start(at(acc, top + z * qz + wrap(x + k, nx) * qx, qx), rq2.at[h, k - 1], next_x(k))
            return group

        def p3():
            mine = row(x * px + z * pz, pz)
            total = acc[h, mine, :]
            for k in range(nz - 1):
                total = total + rp2[h, k]
            O[h, mine, :] = total.astype(jnp.bfloat16)
            group = Group(bytes_of(O, (nz - 1) * pz), bytes_of(O, (nz - 1) * pz))
            piece = at(O, x * px + z * pz, pz)
            for k in range(1, nz):
                group.start(piece, piece, next_z(k))
            return group

        def q3():
            mine = row(top + z * qz + x * qx, qx)
            total = acc[h, mine, :]
            for k in range(nx - 1):
                total = total + rq2[h, k]
            O[h, mine, :] = total.astype(jnp.bfloat16)
            group = Group(bytes_of(O, (nx - 1) * qx), bytes_of(O, (nx - 1) * qx))
            piece = at(O, top + z * qz + x * qx, qx)
            for k in range(1, nx):
                group.start(piece, piece, next_x(k))
            return group

        def p4():
            group = Group(bytes_of(O, (nx - 1) * px), bytes_of(O, (nx - 1) * px))
            piece = at(O, x * px, px)
            for k in range(1, nx):
                group.start(piece, piece, next_x(k))
            return group

        def q4():
            group = Group(bytes_of(O, (nz - 1) * qz), bytes_of(O, (nz - 1) * qz))
            piece = at(O, top + z * qz, qz)
            for k in range(1, nz):
                group.start(piece, piece, next_z(k))
            return group

        p, q = p1(), q1()
        yield
        p.wait_recv()
        p = p2()
        q.wait_recv()
        q = q2()
        yield
        q.wait_recv()
        q = q3()
        p.wait_recv()
        p = p3()
        yield
        q.wait_recv()
        q = q4()
        p.wait_recv()
        p = p4()
        yield
        p.wait_recv()
        q.wait_recv()
        yield

    def columns(table, i, cc, plane):
        at = row((plane * 2 + cc) * width, width)
        sel = jnp.concatenate([table[i, cc, ids_ref[mem, k]] for k in range(SEL)], axis=0)
        V[:, at] = jnp.dot(w_ref[...], sel, preferred_element_type=jnp.float32).astype(jnp.bfloat16)
        GW[...] += lax.dot_general(
            g_ref[:, at], sel, (((1,), (1,)), ((), ())), preferred_element_type=jnp.float32
        )

    def own_column(k, _):
        i, cc = k // 2, k % 2
        columns(T, i, cc, (y + jnp.where(i == 0, 0, i + 1)) % ny)
        return 0

    def near_column(k, _):
        i, cc = k // 2, k % 2
        columns(N, i, cc, (y + jnp.where(i == 0, 1, ny - 1)) % ny)
        return 0

    g1.wait_recv()
    sib_w.wait_recv()
    for g in g_own:
        g.wait()
    grad(0)
    first = reduction(0)
    next(first)
    az_step(3)
    bx_step(3)
    bx_step(4)
    next(first)
    g2.wait_recv()
    grad(1)
    second = reduction(1)
    next(second)
    near = [
        one(table_ref, N.at[0, c], next_y(-1)),
        one(table_ref, N.at[1, c], next_y(1)),
    ]
    next(first)
    az_step(4)
    bx_short.wait_recv()
    t_sib(bx_chunk(minus, 1))
    next(first)
    bx_last.wait_recv()
    t_sib(bx_chunk(s, 2))
    for k in (1,):
        t_sib(bx_chunk(s, k))
    next(second)
    next(first)
    t_out = [
        pltpu.make_async_copy(O.at[h], tout_ref.at[:, h * HALF:(h + 1) * HALF], local.at[3 + h])
        for h in range(2)
    ]
    t_out[0].start()
    own.wait()
    sib_t.wait_recv()
    GW[...] = jnp.zeros_like(GW)
    lax.fori_loop(0, 2 * (1 + far), own_column, 0)
    next(second)
    sib_n = Group(N.at[:, c], N.at[:, 1 - c])
    for i in range(2):
        near[i].wait_recv()
        sib_n.start(N.at[i, c], N.at[i, c], sib)
    next(second)
    sib_n.wait_recv()
    lax.fori_loop(0, 4, near_column, 0)
    v_out = pltpu.make_async_copy(V, vout_ref, local.at[5])
    v_out.start()
    gw_ref[...] = GW[...].astype(jnp.bfloat16)
    next(second)
    t_out[1].start()
    for group in ends:
        group.wait_send()
    v_out.wait()
    for t in t_out:
        t.wait()
    assert used[0] <= N_SEMS, used[0]


def shards(nx, ny, nz, table, block_ids, weights, grad_out):
    rows, width = table.shape
    n_mem = 2 * ny
    blocks = rows // BLOCK
    hit = block_ids[None, :, :] == jnp.arange(blocks, dtype=jnp.int32)[:, None, None]
    at = jnp.arange(n_mem, dtype=jnp.int32)[:, None] * SEL + jnp.arange(SEL, dtype=jnp.int32)[None, :]
    idx = jnp.min(jnp.where(hit, at[None], n_mem * SEL), axis=-1)
    top = rows // 2
    vmem = pl.BlockSpec(memory_space=pltpu.VMEM)
    smem = pl.BlockSpec(memory_space=pltpu.SMEM)
    hbm = pl.BlockSpec(memory_space=pl.ANY)
    return pl.pallas_call(
        functools.partial(kernel, nx, ny, nz, rows, width),
        out_shape=(
            jax.ShapeDtypeStruct(grad_out.shape, jnp.bfloat16),
            jax.ShapeDtypeStruct(weights.shape, jnp.bfloat16),
            jax.ShapeDtypeStruct(table.shape, jnp.bfloat16),
        ),
        in_specs=[smem, smem, hbm, vmem, vmem],
        out_specs=(hbm, vmem, hbm),
        scratch_shapes=[
            pltpu.VMEM((ny - 2, 2, blocks, BLOCK, width), jnp.bfloat16),
            pltpu.VMEM((2, 2, blocks, BLOCK, width), jnp.bfloat16),
            pltpu.VMEM((n_mem * SEL + 1, BLOCK, TILE), jnp.bfloat16),
            pltpu.VMEM((2, n_mem, TILE, HALF), jnp.bfloat16),
            pltpu.VMEM((2, rows, HALF), jnp.float32),
            pltpu.VMEM((2, nx - 1, top // nx, HALF), jnp.float32),
            pltpu.VMEM((2, nz - 1, top // (nx * nz), HALF), jnp.float32),
            pltpu.VMEM((2, nz - 1, top // nz, HALF), jnp.float32),
            pltpu.VMEM((2, nx - 1, top // (nx * nz), HALF), jnp.float32),
            pltpu.VMEM((2, rows, HALF), jnp.bfloat16),
            pltpu.VMEM(grad_out.shape, jnp.bfloat16),
            pltpu.VMEM(weights.shape, jnp.float32),
            pltpu.SemaphoreType.DMA((N_SEMS,)),
            pltpu.SemaphoreType.DMA((N_SEMS,)),
            pltpu.SemaphoreType.DMA((6,)),
        ],
        compiler_params=pltpu.CompilerParams(
            collective_id=0, has_side_effects=True, vmem_limit_bytes=56 * 1024 * 1024
        ),
    )(block_ids, idx, table.reshape(blocks, BLOCK, width), weights, grad_out)


def solution(mesh):
    nx = NX
    nz = mesh.shape["dp"] // nx
    ny = mesh.shape["mem"] // 2
    return jax.shard_map(
        functools.partial(shards, nx, ny, nz),
        mesh=mesh,
        in_specs=(P(None, "mem"), P("dp", None), P(("dp", "mem"), None), P(("dp", "mem"), None)),
        out_specs=(P(("dp", "mem"), None), P(("dp", "mem"), None), P(None, "mem")),
        check_vma=False,
    )
```

```python
import functools

import jax
import jax.numpy as jnp
from jax import lax
from jax.experimental import pallas as pl
from jax.experimental.pallas import tpu as pltpu
from jax.sharding import PartitionSpec as P

MESH = pl.DeviceIdType.MESH
BLOCK = 128
SEL = 4
TILE = 128
HALF = 128
NX = 4
N_SEMS = 72


def kernel(
    nx, ny, nz, rows, width,
    ids_ref, ids_vmem, table_ref, w_ref, g_ref,
    vout_ref, gw_ref, tout_ref,
    T, N, idx_vmem, idx_ref, Wt, Gr, acc, rp1, rp2, rq1, rq2, O, V, GW,
    send, recv, local,
):
    dp, mem = lax.axis_index("dp"), lax.axis_index("mem")
    z, x = dp // nx, dp % nx
    y, c = mem // 2, mem % 2
    s = 1 - 2 * c
    n_mem = 2 * ny
    blocks = rows // BLOCK
    zero_slot = n_mem * SEL
    far = ny - 3
    na = 2 * far // 5
    xr, zr, sh = rows // nx, rows // nz, rows // (nx * nz)
    lx, lz, ly = nx // 2, nz // 2, ny // 2

    def dev(xx, yy, zz, cc):
        return (zz * nx + xx, yy * 2 + cc)

    sib = dev(x, y, z, 1 - c)

    def wrap(v, n):
        return (v + 4 * n) % n

    def row(start, size):
        return pl.ds(pl.multiple_of(start, size), size)

    def rows_of(ref, lead, start, size):
        if size >= BLOCK:
            return ref.at[(*lead, pl.ds(start // BLOCK, size // BLOCK))]
        return ref.at[(*lead, start // BLOCK, row(start % BLOCK, size))]

    def next_x(d):
        return dev(wrap(x + d, nx), y, z, c)

    def next_y(d):
        return dev(x, wrap(y + d, ny), z, c)

    def next_z(d):
        return dev(x, y, wrap(z + d, nz), c)

    used = [0]
    ends = []

    class Group:
        def __init__(self, out=None, into=None):
            self.k = used[0]
            used[0] += 1
            self.out, self.into = out, into
            ends.append(self)

        def start(self, src, dst, device):
            copy = pltpu.make_async_remote_copy(
                src_ref=src, dst_ref=dst, send_sem=send.at[self.k], recv_sem=recv.at[self.k],
                device_id=device, device_id_type=MESH,
            )
            copy.start()
            if self.out is None:
                self.out = src
            if self.into is None:
                self.into = dst
            return self

        def wait_recv(self):
            pltpu.make_async_copy(self.into, self.into, recv.at[self.k]).wait()

        def wait_send(self):
            pltpu.make_async_copy(self.out, self.out, send.at[self.k]).wait()

    def one(src, dst, device):
        return Group().start(src, dst, device)

    own = pltpu.make_async_copy(table_ref, T.at[0, c], local.at[0])
    own.start()
    g_own = [
        pltpu.make_async_copy(g_ref.at[:, row(mem * width + h * HALF, HALF)], Gr.at[h, mem], local.at[1 + h])
        for h in range(2)
    ]
    for g in g_own:
        g.start()
    barrier = pltpu.get_barrier_semaphore()
    peers = [(min(k // 2, ny - k // 2), (dp, (mem + k) % n_mem)) for k in range(1, n_mem)]
    peers += [(min(k, nx - k), next_x(k)) for k in range(1, nx)]
    peers += [(min(k, nz - k), next_z(k)) for k in range(1, nz)]
    peers = [p for _, p in sorted(peers, key=lambda p: -p[0])]
    for p in peers:
        pl.semaphore_signal(barrier, inc=1, device_id=p, device_id_type=MESH)
    tile_at = lax.broadcasted_iota(jnp.int32, (blocks, n_mem), 1) * SEL
    block_at = lax.broadcasted_iota(jnp.int32, (blocks, n_mem), 0)
    found = jnp.full((blocks, n_mem), zero_slot, jnp.int32)
    for k in range(SEL):
        found = jnp.where(ids_vmem[k:k + 1, :] == block_at, tile_at + k, found)
    idx_vmem[...] = found
    idx_copy = pltpu.make_async_copy(idx_vmem, idx_ref, local.at[6])
    idx_copy.start()
    Wt[zero_slot] = jnp.zeros((BLOCK, TILE), jnp.bfloat16)
    for k in range(SEL):
        Wt[mem * SEL + k] = w_ref[:, k * BLOCK:(k + 1) * BLOCK].astype(jnp.float32).T.astype(jnp.bfloat16)
    pl.semaphore_wait(barrier, len(peers))

    share_a, share_b = z * zr + x * sh, x * xr + z * sh
    a_planes, b_planes = slice(1, 1 + na), slice(1 + na, 1 + far)
    in_a = rows_of(T, (a_planes, c), share_a, sh)
    in_b = rows_of(T, (b_planes, c), share_b, sh)
    shares_a, shares_b = Group(in_a, in_a), Group(in_b, in_b)
    for i in sorted(range(1, 1 + far), key=lambda i: min(i + 1, ny - i - 1)):
        group, at = (shares_a, share_a) if i <= na else (shares_b, share_b)
        group.start(rows_of(table_ref, (), at, sh), rows_of(T, (i, c), at, sh), next_y(-(i + 1)))

    def w_piece(d, back):
        return Wt.at[pl.ds((wrap(y - d * back, ny) * 2 + c) * SEL, SEL)]

    def w_hop(d, h):
        p = w_piece(d, h - 1)
        return one(p, p, next_y(d))

    all_w = Wt.at[0:ny * SEL]
    sib_w = Group(all_w, all_w)

    def w_sib(d, back):
        p = w_piece(d, back)
        sib_w.start(p, p, sib)

    wl, ws = w_hop(s, 1), w_hop(-s, 1)
    w_sib(s, 0)
    sib_t = Group(T.at[:, c], T.at[:, 1 - c])
    sib_t.start(table_ref, T.at[0, c], sib)

    def t_sib(p):
        sib_t.start(p, p, sib)

    g_order = sorted(range(1, n_mem), key=lambda k: -min(k // 2, ny - k // 2))
    g_halves = [Group(Gr.at[h, 0:n_mem - 1], Gr.at[h, 0:n_mem - 1]) for h in range(2)]

    def g_send(h, lo, hi):
        for k in g_order[lo:hi]:
            m = (mem + k) % n_mem
            g_halves[h].start(g_ref.at[:, row(m * width + h * HALF, HALF)], Gr.at[h, mem], (dp, m))

    g1, g2 = g_halves

    def ax_piece(back):
        return rows_of(T, (a_planes, c), z * zr + wrap(x - back, nx) * sh, sh)

    def az_piece(i, d, back):
        return rows_of(T, (i, c), wrap(z - d * back, nz) * zr, zr)

    def az_chunk(d, back):
        return rows_of(T, (a_planes, c), wrap(z - d * back, nz) * zr, zr)

    def b_piece(dx, xback, dz, zback):
        return rows_of(T, (b_planes, c), wrap(x - dx * xback, nx) * xr + wrap(z - dz * zback, nz) * sh, sh)

    def bx_chunk(d, back):
        return rows_of(T, (b_planes, c), wrap(x - d * back, nx) * xr, xr)

    def bz_hop(d, h):
        p = b_piece(s, 0, d, h - 1)
        return one(p, p, next_z(d))

    bx_short = Group(bx_chunk(-s, 0), bx_chunk(-s, 1))
    bx_last = Group(bx_chunk(s, 1), bx_chunk(s, 2))
    bx_first = {}

    def bx_start(d, back):
        p = b_piece(s, 0, d, back)
        bx_first[(d is s, back)] = one(p, p, next_x(s))
        bx_short.start(p, p, next_x(-s))

    def bx_forward(d, back):
        bx_first[(d is s, back)].wait_recv()
        p = b_piece(s, 1, d, back)
        bx_last.start(p, p, next_x(s))

    minus = -s
    bzl = bzs = None
    azl, azs = {}, {}

    def az_step(h):
        if h > lz:
            return
        for i in range(1, 1 + na):
            if h > 0:
                azl[i].wait_recv()
            if h < lz:
                p = az_piece(i, s, h)
                azl[i] = one(p, p, next_z(s))
            if 0 < h < lz:
                azs[i].wait_recv()
            if h < lz - 1:
                p = az_piece(i, minus, h)
                azs[i] = one(p, p, next_z(minus))
        t_sib(az_chunk(s, h))
        if 0 < h < lz:
            t_sib(az_chunk(minus, h))

    def w_step(h):
        nonlocal wl, ws
        if h > ly:
            return
        wl.wait_recv()
        if h < ly:
            wl = w_hop(s, h + 1)
        w_sib(s, h)
        if h < ly:
            ws.wait_recv()
            if h < ly - 1:
                ws = w_hop(minus, h + 1)
            w_sib(minus, h)

    def bz_step(h):
        nonlocal bzl, bzs
        if h > lz:
            return
        bzl.wait_recv()
        if h < lz:
            bzl = bz_hop(s, h + 1)
        bx_start(s, h)
        if h < lz:
            bzs.wait_recv()
            if h < lz - 1:
                bzs = bz_hop(minus, h + 1)
            bx_start(minus, h)

    def bx_step(h):
        if h > lz:
            return
        bx_forward(s, h)
        if 0 < h < lz:
            bx_forward(minus, h)

    def grad(h):
        def grad_rows(i, _):
            parts = []
            for b in range(2):
                parts.append(
                    jnp.concatenate([Wt[idx_ref[2 * i + b, t]] for t in range(n_mem)], axis=1)
                )
            lhs = jnp.concatenate(parts, axis=0)
            rhs = Gr[h].reshape(n_mem * TILE, HALF)
            r = jnp.dot(lhs, rhs, preferred_element_type=jnp.float32)
            acc[h, row(i * 2 * BLOCK, 2 * BLOCK), :] = r
            return 0

        lax.fori_loop(0, blocks // 2, grad_rows, 0)

    top = 3 * rows // 4
    px, pz = top // nx, top // (nx * nz)
    qz, qx = (rows - top) // nz, (rows - top) // (nx * nz)

    def reduction(h):
        def at(ref, start, size):
            return ref.at[h, row(start, size), :]

        def bytes_of(ref, size):
            return ref.at[h, 0:size, :]

        def p1():
            group = Group(rp1.at[h], rp1.at[h])
            for k in range(1, nx):
                group.start(at(acc, wrap(x + k, nx) * px, px), rp1.at[h, k - 1], next_x(k))
            return group

        def q1():
            group = Group(rq1.at[h], rq1.at[h])
            for k in range(1, nz):
                group.start(at(acc, top + wrap(z + k, nz) * qz, qz), rq1.at[h, k - 1], next_z(k))
            return group

        def p2():
            mine = row(x * px, px)
            total = acc[h, mine, :]
            for k in range(nx - 1):
                total = total + rp1[h, k]
            acc[h, mine, :] = total
            group = Group(rp2.at[h], rp2.at[h])
            for k in range(1, nz):
                group.start(at(acc, x * px + wrap(z + k, nz) * pz, pz), rp2.at[h, k - 1], next_z(k))
            return group

        def q2():
            mine = row(top + z * qz, qz)
            total = acc[h, mine, :]
            for k in range(nz - 1):
                total = total + rq1[h, k]
            acc[h, mine, :] = total
            group = Group(rq2.at[h], rq2.at[h])
            for k in range(1, nx):
                group.start(at(acc, top + z * qz + wrap(x + k, nx) * qx, qx), rq2.at[h, k - 1], next_x(k))
            return group

        def p3():
            mine = row(x * px + z * pz, pz)
            total = acc[h, mine, :]
            for k in range(nz - 1):
                total = total + rp2[h, k]
            O[h, mine, :] = total.astype(jnp.bfloat16)
            group = Group(bytes_of(O, (nz - 1) * pz), bytes_of(O, (nz - 1) * pz))
            piece = at(O, x * px + z * pz, pz)
            for k in range(1, nz):
                group.start(piece, piece, next_z(k))
            return group

        def q3():
            mine = row(top + z * qz + x * qx, qx)
            total = acc[h, mine, :]
            for k in range(nx - 1):
                total = total + rq2[h, k]
            O[h, mine, :] = total.astype(jnp.bfloat16)
            group = Group(bytes_of(O, (nx - 1) * qx), bytes_of(O, (nx - 1) * qx))
            piece = at(O, top + z * qz + x * qx, qx)
            for k in range(1, nx):
                group.start(piece, piece, next_x(k))
            return group

        def p4():
            group = Group(bytes_of(O, (nx - 1) * px), bytes_of(O, (nx - 1) * px))
            piece = at(O, x * px, px)
            for k in range(1, nx):
                group.start(piece, piece, next_x(k))
            return group

        def q4():
            group = Group(bytes_of(O, (nz - 1) * qz), bytes_of(O, (nz - 1) * qz))
            piece = at(O, top + z * qz, qz)
            for k in range(1, nz):
                group.start(piece, piece, next_z(k))
            return group

        p, q = p1(), q1()
        yield
        p.wait_recv()
        p = p2()
        q.wait_recv()
        q = q2()
        yield
        q.wait_recv()
        q = q3()
        p.wait_recv()
        p = p3()
        yield
        q.wait_recv()
        q = q4()
        p.wait_recv()
        p = p4()
        yield
        p.wait_recv()
        q.wait_recv()
        yield

    def columns(table, i, cc, plane):
        at = row((plane * 2 + cc) * width, width)
        sel = jnp.concatenate([table[i, cc, ids_ref[k, mem]] for k in range(SEL)], axis=0)
        V[:, at] = jnp.dot(w_ref[...], sel, preferred_element_type=jnp.float32).astype(jnp.bfloat16)
        GW[...] += lax.dot_general(
            g_ref[:, at], sel, (((1,), (1,)), ((), ())), preferred_element_type=jnp.float32
        )

    def own_column(k, _):
        i, cc = k // 2, k % 2
        columns(T, i, cc, (y + jnp.where(i == 0, 0, i + 1)) % ny)
        return 0

    def near_column(k, _):
        i, cc = k // 2, k % 2
        columns(N, i, cc, (y + jnp.where(i == 0, 1, ny - 1)) % ny)
        return 0

    def near_start():
        return [
            one(table_ref, N.at[0, c], next_y(-1)),
            one(table_ref, N.at[1, c], next_y(1)),
        ]

    w_step(1)
    g_send(0, 0, 4)
    shares_a.wait_recv()
    ax = []
    for k in range(1, nx):
        p = ax_piece(0)
        ax.append(one(p, p, next_x(k)))
    shares_b.wait_recv()
    bzl, bzs = bz_hop(s, 1), bz_hop(minus, 1) if lz > 1 else None
    bx_start(s, 0)

    w_step(2)
    g_send(0, 4, 8)
    bz_step(1)
    for r in ax:
        r.wait_recv()
    az_step(0)
    w_step(3)
    g_send(0, 8, n_mem)
    bz_step(2)
    bx_step(0)
    w_step(4)
    g_send(1, 0, n_mem)
    az_step(1)
    bz_step(3)
    bx_step(1)
    g1.wait_recv()
    sib_w.wait_recv()
    for g in g_own:
        g.wait()
    idx_copy.wait()
    grad(0)
    first = reduction(0)
    next(first)
    near = near_start()
    bz_step(4)
    t_sib(bx_chunk(s, 0))
    az_step(2)
    bx_step(2)
    next(first)
    bx_step(3)
    g2.wait_recv()
    grad(1)
    second = reduction(1)
    next(second)
    next(first)
    az_step(3)
    bx_step(4)
    t_sib(bx_chunk(s, 1))
    next(second)
    next(first)
    az_step(4)
    bx_short.wait_recv()
    t_sib(bx_chunk(minus, 1))
    bx_last.wait_recv()
    t_sib(bx_chunk(s, 2))
    next(second)
    next(first)
    t_out = [
        pltpu.make_async_copy(O.at[h], tout_ref.at[:, h * HALF:(h + 1) * HALF], local.at[3 + h])
        for h in range(2)
    ]
    t_out[0].start()
    own.wait()
    sib_t.wait_recv()
    GW[...] = jnp.zeros_like(GW)
    lax.fori_loop(0, 2 * (1 + far), own_column, 0)
    next(second)
    sib_n = Group(N.at[:, c], N.at[:, 1 - c])
    for i in range(2):
        near[i].wait_recv()
        sib_n.start(N.at[i, c], N.at[i, c], sib)
    sib_n.wait_recv()
    lax.fori_loop(0, 4, near_column, 0)
    v_out = pltpu.make_async_copy(V, vout_ref, local.at[5])
    v_out.start()
    gw_ref[...] = GW[...].astype(jnp.bfloat16)
    next(second)
    t_out[1].start()
    for group in ends:
        group.wait_send()
    v_out.wait()
    for t in t_out:
        t.wait()
    assert used[0] <= N_SEMS, used[0]


def shards(nx, ny, nz, table, block_ids, weights, grad_out):
    rows, width = table.shape
    n_mem = 2 * ny
    blocks = rows // BLOCK
    top = 3 * rows // 4
    vmem = pl.BlockSpec(memory_space=pltpu.VMEM)
    smem = pl.BlockSpec(memory_space=pltpu.SMEM)
    hbm = pl.BlockSpec(memory_space=pl.ANY)
    return pl.pallas_call(
        functools.partial(kernel, nx, ny, nz, rows, width),
        out_shape=(
            jax.ShapeDtypeStruct(grad_out.shape, jnp.bfloat16),
            jax.ShapeDtypeStruct(weights.shape, jnp.bfloat16),
            jax.ShapeDtypeStruct(table.shape, jnp.bfloat16),
        ),
        in_specs=[smem, vmem, hbm, vmem, vmem],
        out_specs=(hbm, vmem, hbm),
        scratch_shapes=[
            pltpu.VMEM((ny - 2, 2, blocks, BLOCK, width), jnp.bfloat16),
            pltpu.VMEM((2, 2, blocks, BLOCK, width), jnp.bfloat16),
            pltpu.VMEM((blocks, n_mem), jnp.int32),
            pltpu.SMEM((blocks, n_mem), jnp.int32),
            pltpu.VMEM((n_mem * SEL + 1, BLOCK, TILE), jnp.bfloat16),
            pltpu.VMEM((2, n_mem, TILE, HALF), jnp.bfloat16),
            pltpu.VMEM((2, rows, HALF), jnp.float32),
            pltpu.VMEM((2, nx - 1, top // nx, HALF), jnp.float32),
            pltpu.VMEM((2, nz - 1, top // (nx * nz), HALF), jnp.float32),
            pltpu.VMEM((2, nz - 1, (rows - top) // nz, HALF), jnp.float32),
            pltpu.VMEM((2, nx - 1, (rows - top) // (nx * nz), HALF), jnp.float32),
            pltpu.VMEM((2, rows, HALF), jnp.bfloat16),
            pltpu.VMEM(grad_out.shape, jnp.bfloat16),
            pltpu.VMEM(weights.shape, jnp.float32),
            pltpu.SemaphoreType.DMA((N_SEMS,)),
            pltpu.SemaphoreType.DMA((N_SEMS,)),
            pltpu.SemaphoreType.DMA((7,)),
        ],
        compiler_params=pltpu.CompilerParams(
            collective_id=0, has_side_effects=True, vmem_limit_bytes=56 * 1024 * 1024
        ),
    )(block_ids.T, block_ids.T, table.reshape(blocks, BLOCK, width), weights, grad_out)


def solution(mesh):
    nx = NX
    nz = mesh.shape["dp"] // nx
    ny = mesh.shape["mem"] // 2
    return jax.shard_map(
        functools.partial(shards, nx, ny, nz),
        mesh=mesh,
        in_specs=(P(None, "mem"), P("dp", None), P(("dp", "mem"), None), P(("dp", "mem"), None)),
        out_specs=(P(("dp", "mem"), None), P(("dp", "mem"), None), P(None, "mem")),
        check_vma=False,
    )
```

```python
import functools

import jax
import jax.numpy as jnp
from jax import lax
from jax.experimental import pallas as pl
from jax.experimental.pallas import tpu as pltpu
from jax.sharding import PartitionSpec as P

MESH = pl.DeviceIdType.MESH
BLOCK = 128
SEL = 4
TILE = 128
HALF = 128
NX = 4
N_SEMS = 72


def kernel(
    nx, ny, nz, rows, width,
    ids_ref, ids_vmem, table_ref, w_ref, g_ref,
    vout_ref, gw_ref, tout_ref,
    T, N, idx_vmem, idx_ref, Wt, Gr, acc, rp1, rp2, rq1, rq2, O, V, GW,
    send, recv, local,
):
    dp, mem = lax.axis_index("dp"), lax.axis_index("mem")
    z, x = dp // nx, dp % nx
    y, c = mem // 2, mem % 2
    s = 1 - 2 * c
    n_mem = 2 * ny
    blocks = rows // BLOCK
    zero_slot = n_mem * SEL
    far = ny - 3
    na = 2 * far // 5
    xr, zr, sh = rows // nx, rows // nz, rows // (nx * nz)
    lx, lz, ly = nx // 2, nz // 2, ny // 2

    def dev(xx, yy, zz, cc):
        return (zz * nx + xx, yy * 2 + cc)

    sib = dev(x, y, z, 1 - c)

    def wrap(v, n):
        return (v + 4 * n) % n

    def row(start, size):
        return pl.ds(pl.multiple_of(start, size), size)

    def rows_of(ref, lead, start, size):
        if size >= BLOCK:
            return ref.at[(*lead, pl.ds(start // BLOCK, size // BLOCK))]
        return ref.at[(*lead, start // BLOCK, row(start % BLOCK, size))]

    def next_x(d):
        return dev(wrap(x + d, nx), y, z, c)

    def next_y(d):
        return dev(x, wrap(y + d, ny), z, c)

    def next_z(d):
        return dev(x, y, wrap(z + d, nz), c)

    used = [0]
    ends = []

    class Group:
        def __init__(self, out=None, into=None):
            self.k = used[0]
            used[0] += 1
            self.out, self.into = out, into
            ends.append(self)

        def start(self, src, dst, device):
            copy = pltpu.make_async_remote_copy(
                src_ref=src, dst_ref=dst, send_sem=send.at[self.k], recv_sem=recv.at[self.k],
                device_id=device, device_id_type=MESH,
            )
            copy.start()
            if self.out is None:
                self.out = src
            if self.into is None:
                self.into = dst
            return self

        def wait_recv(self):
            pltpu.make_async_copy(self.into, self.into, recv.at[self.k]).wait()

        def wait_send(self):
            pltpu.make_async_copy(self.out, self.out, send.at[self.k]).wait()

    def one(src, dst, device):
        return Group().start(src, dst, device)

    own = pltpu.make_async_copy(table_ref, T.at[0, c], local.at[0])
    own.start()
    g_own = [
        pltpu.make_async_copy(g_ref.at[:, row(mem * width + h * HALF, HALF)], Gr.at[h, mem], local.at[1 + h])
        for h in range(2)
    ]
    for g in g_own:
        g.start()
    barrier = pltpu.get_barrier_semaphore()
    peers = [(min(k // 2, ny - k // 2), (dp, (mem + k) % n_mem)) for k in range(1, n_mem)]
    peers += [(min(k, nx - k), next_x(k)) for k in range(1, nx)]
    peers += [(min(k, nz - k), next_z(k)) for k in range(1, nz)]
    peers = [p for _, p in sorted(peers, key=lambda p: -p[0])]
    for p in peers:
        pl.semaphore_signal(barrier, inc=1, device_id=p, device_id_type=MESH)
    tile_at = lax.broadcasted_iota(jnp.int32, (blocks, n_mem), 1) * SEL
    block_at = lax.broadcasted_iota(jnp.int32, (blocks, n_mem), 0)
    found = jnp.full((blocks, n_mem), zero_slot, jnp.int32)
    for k in range(SEL):
        found = jnp.where(ids_vmem[k:k + 1, :] == block_at, tile_at + k, found)
    idx_vmem[...] = found
    idx_copy = pltpu.make_async_copy(idx_vmem, idx_ref, local.at[6])
    idx_copy.start()
    Wt[zero_slot] = jnp.zeros((BLOCK, TILE), jnp.bfloat16)
    for k in range(SEL):
        Wt[mem * SEL + k] = w_ref[:, k * BLOCK:(k + 1) * BLOCK].astype(jnp.float32).T.astype(jnp.bfloat16)
    pl.semaphore_wait(barrier, len(peers))

    share_a, share_b = z * zr + x * sh, x * xr + z * sh
    a_planes, b_planes = slice(1, 1 + na), slice(1 + na, 1 + far)
    in_a = rows_of(T, (a_planes, c), share_a, sh)
    in_b = rows_of(T, (b_planes, c), share_b, sh)
    shares_a, shares_b = Group(in_a, in_a), Group(in_b, in_b)
    for i in sorted(range(1, 1 + far), key=lambda i: min(i + 1, ny - i - 1)):
        group, at = (shares_a, share_a) if i <= na else (shares_b, share_b)
        group.start(rows_of(table_ref, (), at, sh), rows_of(T, (i, c), at, sh), next_y(-(i + 1)))

    def w_piece(d, back):
        return Wt.at[pl.ds((wrap(y - d * back, ny) * 2 + c) * SEL, SEL)]

    def w_hop(d, h):
        p = w_piece(d, h - 1)
        return one(p, p, next_y(d))

    all_w = Wt.at[0:ny * SEL]
    sib_w = Group(all_w, all_w)

    def w_sib(d, back):
        p = w_piece(d, back)
        sib_w.start(p, p, sib)

    wl, ws = w_hop(s, 1), w_hop(-s, 1)
    w_sib(s, 0)
    sib_t = Group(T.at[:, c], T.at[:, 1 - c])
    sib_t.start(table_ref, T.at[0, c], sib)

    def t_sib(p):
        sib_t.start(p, p, sib)

    g_order = sorted(range(1, n_mem), key=lambda k: -min(k // 2, ny - k // 2))
    g_halves = [Group(Gr.at[h, 0:n_mem - 1], Gr.at[h, 0:n_mem - 1]) for h in range(2)]

    def g_send(h, lo, hi):
        for k in g_order[lo:hi]:
            m = (mem + k) % n_mem
            g_halves[h].start(g_ref.at[:, row(m * width + h * HALF, HALF)], Gr.at[h, mem], (dp, m))

    g1, g2 = g_halves

    def ax_piece(back):
        return rows_of(T, (a_planes, c), z * zr + wrap(x - back, nx) * sh, sh)

    def az_piece(i, d, back):
        return rows_of(T, (i, c), wrap(z - d * back, nz) * zr, zr)

    def az_chunk(d, back):
        return rows_of(T, (a_planes, c), wrap(z - d * back, nz) * zr, zr)

    def b_piece(dx, xback, dz, zback):
        return rows_of(T, (b_planes, c), wrap(x - dx * xback, nx) * xr + wrap(z - dz * zback, nz) * sh, sh)

    def bx_chunk(d, back):
        return rows_of(T, (b_planes, c), wrap(x - d * back, nx) * xr, xr)

    def bz_hop(d, h):
        p = b_piece(s, 0, d, h - 1)
        return one(p, p, next_z(d))

    bx_short = Group(bx_chunk(-s, 0), bx_chunk(-s, 1))
    bx_last = Group(bx_chunk(s, 1), bx_chunk(s, 2))
    bx_first = {}

    def bx_start(d, back):
        p = b_piece(s, 0, d, back)
        bx_first[(d is s, back)] = one(p, p, next_x(s))
        bx_short.start(p, p, next_x(-s))

    def bx_forward(d, back):
        bx_first[(d is s, back)].wait_recv()
        p = b_piece(s, 1, d, back)
        bx_last.start(p, p, next_x(s))

    minus = -s
    bzl = bzs = None
    azl, azs = {}, {}

    def az_step(h):
        if h > lz:
            return
        for i in range(1, 1 + na):
            if h > 0:
                azl[i].wait_recv()
            if h < lz:
                p = az_piece(i, s, h)
                azl[i] = one(p, p, next_z(s))
            if 0 < h < lz:
                azs[i].wait_recv()
            if h < lz - 1:
                p = az_piece(i, minus, h)
                azs[i] = one(p, p, next_z(minus))
        t_sib(az_chunk(s, h))
        if 0 < h < lz:
            t_sib(az_chunk(minus, h))

    def w_step(h):
        nonlocal wl, ws
        if h > ly:
            return
        wl.wait_recv()
        if h < ly:
            wl = w_hop(s, h + 1)
        w_sib(s, h)
        if h < ly:
            ws.wait_recv()
            if h < ly - 1:
                ws = w_hop(minus, h + 1)
            w_sib(minus, h)

    def bz_step(h):
        nonlocal bzl, bzs
        if h > lz:
            return
        bzl.wait_recv()
        if h < lz:
            bzl = bz_hop(s, h + 1)
        bx_start(s, h)
        if h < lz:
            bzs.wait_recv()
            if h < lz - 1:
                bzs = bz_hop(minus, h + 1)
            bx_start(minus, h)

    def bx_step(h):
        if h > lz:
            return
        bx_forward(s, h)
        if 0 < h < lz:
            bx_forward(minus, h)

    def grad(h):
        def grad_rows(i, _):
            parts = []
            for b in range(2):
                parts.append(
                    jnp.concatenate([Wt[idx_ref[2 * i + b, t]] for t in range(n_mem)], axis=1)
                )
            lhs = jnp.concatenate(parts, axis=0)
            rhs = Gr[h].reshape(n_mem * TILE, HALF)
            r = jnp.dot(lhs, rhs, preferred_element_type=jnp.float32)
            acc[h, row(i * 2 * BLOCK, 2 * BLOCK), :] = r
            return 0

        lax.fori_loop(0, blocks // 2, grad_rows, 0)

    top = 3 * rows // 4
    px, pz = top // nx, top // (nx * nz)
    qz, qx = (rows - top) // nz, (rows - top) // (nx * nz)

    def reduction(h):
        def at(ref, start, size):
            return ref.at[h, row(start, size), :]

        def bytes_of(ref, size):
            return ref.at[h, 0:size, :]

        def p1():
            group = Group(rp1.at[h], rp1.at[h])
            for k in range(1, nx):
                group.start(at(acc, wrap(x + k, nx) * px, px), rp1.at[h, k - 1], next_x(k))
            return group

        def q1():
            group = Group(rq1.at[h], rq1.at[h])
            for k in range(1, nz):
                group.start(at(acc, top + wrap(z + k, nz) * qz, qz), rq1.at[h, k - 1], next_z(k))
            return group

        def p2():
            mine = row(x * px, px)
            total = acc[h, mine, :]
            for k in range(nx - 1):
                total = total + rp1[h, k]
            acc[h, mine, :] = total
            group = Group(rp2.at[h], rp2.at[h])
            for k in range(1, nz):
                group.start(at(acc, x * px + wrap(z + k, nz) * pz, pz), rp2.at[h, k - 1], next_z(k))
            return group

        def q2():
            mine = row(top + z * qz, qz)
            total = acc[h, mine, :]
            for k in range(nz - 1):
                total = total + rq1[h, k]
            acc[h, mine, :] = total
            group = Group(rq2.at[h], rq2.at[h])
            for k in range(1, nx):
                group.start(at(acc, top + z * qz + wrap(x + k, nx) * qx, qx), rq2.at[h, k - 1], next_x(k))
            return group

        def p3():
            mine = row(x * px + z * pz, pz)
            total = acc[h, mine, :]
            for k in range(nz - 1):
                total = total + rp2[h, k]
            O[h, mine, :] = total.astype(jnp.bfloat16)
            group = Group(bytes_of(O, (nz - 1) * pz), bytes_of(O, (nz - 1) * pz))
            piece = at(O, x * px + z * pz, pz)
            for k in range(1, nz):
                group.start(piece, piece, next_z(k))
            return group

        def q3():
            mine = row(top + z * qz + x * qx, qx)
            total = acc[h, mine, :]
            for k in range(nx - 1):
                total = total + rq2[h, k]
            O[h, mine, :] = total.astype(jnp.bfloat16)
            group = Group(bytes_of(O, (nx - 1) * qx), bytes_of(O, (nx - 1) * qx))
            piece = at(O, top + z * qz + x * qx, qx)
            for k in range(1, nx):
                group.start(piece, piece, next_x(k))
            return group

        def p4():
            group = Group(bytes_of(O, (nx - 1) * px), bytes_of(O, (nx - 1) * px))
            piece = at(O, x * px, px)
            for k in range(1, nx):
                group.start(piece, piece, next_x(k))
            return group

        def q4():
            group = Group(bytes_of(O, (nz - 1) * qz), bytes_of(O, (nz - 1) * qz))
            piece = at(O, top + z * qz, qz)
            for k in range(1, nz):
                group.start(piece, piece, next_z(k))
            return group

        p, q = p1(), q1()
        yield
        p.wait_recv()
        p = p2()
        q.wait_recv()
        q = q2()
        yield
        q.wait_recv()
        q = q3()
        p.wait_recv()
        p = p3()
        yield
        q.wait_recv()
        q = q4()
        p.wait_recv()
        p = p4()
        yield
        p.wait_recv()
        q.wait_recv()
        yield

    def columns(table, i, cc, plane):
        at = row((plane * 2 + cc) * width, width)
        sel = jnp.concatenate([table[i, cc, ids_ref[k, mem]] for k in range(SEL)], axis=0)
        V[:, at] = jnp.dot(w_ref[...], sel, preferred_element_type=jnp.float32).astype(jnp.bfloat16)
        GW[...] += lax.dot_general(
            g_ref[:, at], sel, (((1,), (1,)), ((), ())), preferred_element_type=jnp.float32
        )

    def own_column(k, _):
        i, cc = k // 2, k % 2
        columns(T, i, cc, (y + jnp.where(i == 0, 0, i + 1)) % ny)
        return 0

    def near_column(k, _):
        i, cc = k // 2, k % 2
        columns(N, i, cc, (y + jnp.where(i == 0, 1, ny - 1)) % ny)
        return 0

    def near_start():
        return [
            one(table_ref, N.at[0, c], next_y(-1)),
            one(table_ref, N.at[1, c], next_y(1)),
        ]

    w_step(1)
    g_send(0, 0, 4)
    shares_a.wait_recv()
    ax = []
    for k in range(1, nx):
        p = ax_piece(0)
        ax.append(one(p, p, next_x(k)))
    shares_b.wait_recv()
    bzl, bzs = bz_hop(s, 1), bz_hop(minus, 1) if lz > 1 else None
    bx_start(s, 0)

    w_step(2)
    g_send(0, 4, 8)
    bz_step(1)
    for r in ax:
        r.wait_recv()
    az_step(0)
    w_step(3)
    g_send(0, 8, n_mem)
    bz_step(2)
    bx_step(0)
    w_step(4)
    g_send(1, 0, n_mem)
    az_step(1)
    bz_step(3)
    bx_step(1)
    g1.wait_recv()
    sib_w.wait_recv()
    for g in g_own:
        g.wait()
    idx_copy.wait()
    grad(0)
    first = reduction(0)
    next(first)
    near = near_start()
    bz_step(4)
    t_sib(bx_chunk(s, 0))
    az_step(2)
    bx_step(2)
    next(first)
    az_step(3)
    bx_step(3)
    g2.wait_recv()
    grad(1)
    second = reduction(1)
    next(second)
    bx_step(4)
    t_sib(bx_chunk(s, 1))
    next(first)
    az_step(4)
    next(second)
    next(first)
    bx_short.wait_recv()
    t_sib(bx_chunk(minus, 1))
    bx_last.wait_recv()
    t_sib(bx_chunk(s, 2))
    next(second)
    next(first)
    t_out = [
        pltpu.make_async_copy(O.at[h], tout_ref.at[:, h * HALF:(h + 1) * HALF], local.at[3 + h])
        for h in range(2)
    ]
    t_out[0].start()
    own.wait()
    sib_t.wait_recv()
    GW[...] = jnp.zeros_like(GW)
    lax.fori_loop(0, 2 * (1 + far), own_column, 0)
    next(second)
    sib_n = Group(N.at[:, c], N.at[:, 1 - c])
    for i in range(2):
        near[i].wait_recv()
        sib_n.start(N.at[i, c], N.at[i, c], sib)
    sib_n.wait_recv()
    lax.fori_loop(0, 4, near_column, 0)
    v_out = pltpu.make_async_copy(V, vout_ref, local.at[5])
    v_out.start()
    gw_ref[...] = GW[...].astype(jnp.bfloat16)
    next(second)
    t_out[1].start()
    for group in ends:
        group.wait_send()
    v_out.wait()
    for t in t_out:
        t.wait()
    assert used[0] <= N_SEMS, used[0]


def shards(nx, ny, nz, table, block_ids, weights, grad_out):
    rows, width = table.shape
    n_mem = 2 * ny
    blocks = rows // BLOCK
    top = 3 * rows // 4
    vmem = pl.BlockSpec(memory_space=pltpu.VMEM)
    smem = pl.BlockSpec(memory_space=pltpu.SMEM)
    hbm = pl.BlockSpec(memory_space=pl.ANY)
    return pl.pallas_call(
        functools.partial(kernel, nx, ny, nz, rows, width),
        out_shape=(
            jax.ShapeDtypeStruct(grad_out.shape, jnp.bfloat16),
            jax.ShapeDtypeStruct(weights.shape, jnp.bfloat16),
            jax.ShapeDtypeStruct(table.shape, jnp.bfloat16),
        ),
        in_specs=[smem, vmem, hbm, vmem, vmem],
        out_specs=(hbm, vmem, hbm),
        scratch_shapes=[
            pltpu.VMEM((ny - 2, 2, blocks, BLOCK, width), jnp.bfloat16),
            pltpu.VMEM((2, 2, blocks, BLOCK, width), jnp.bfloat16),
            pltpu.VMEM((blocks, n_mem), jnp.int32),
            pltpu.SMEM((blocks, n_mem), jnp.int32),
            pltpu.VMEM((n_mem * SEL + 1, BLOCK, TILE), jnp.bfloat16),
            pltpu.VMEM((2, n_mem, TILE, HALF), jnp.bfloat16),
            pltpu.VMEM((2, rows, HALF), jnp.float32),
            pltpu.VMEM((2, nx - 1, top // nx, HALF), jnp.float32),
            pltpu.VMEM((2, nz - 1, top // (nx * nz), HALF), jnp.float32),
            pltpu.VMEM((2, nz - 1, (rows - top) // nz, HALF), jnp.float32),
            pltpu.VMEM((2, nx - 1, (rows - top) // (nx * nz), HALF), jnp.float32),
            pltpu.VMEM((2, rows, HALF), jnp.bfloat16),
            pltpu.VMEM(grad_out.shape, jnp.bfloat16),
            pltpu.VMEM(weights.shape, jnp.float32),
            pltpu.SemaphoreType.DMA((N_SEMS,)),
            pltpu.SemaphoreType.DMA((N_SEMS,)),
            pltpu.SemaphoreType.DMA((7,)),
        ],
        compiler_params=pltpu.CompilerParams(
            collective_id=0, has_side_effects=True, vmem_limit_bytes=56 * 1024 * 1024
        ),
    )(block_ids.T, block_ids.T, table.reshape(blocks, BLOCK, width), weights, grad_out)


def solution(mesh):
    nx = NX
    nz = mesh.shape["dp"] // nx
    ny = mesh.shape["mem"] // 2
    return jax.shard_map(
        functools.partial(shards, nx, ny, nz),
        mesh=mesh,
        in_specs=(P(None, "mem"), P("dp", None), P(("dp", "mem"), None), P(("dp", "mem"), None)),
        out_specs=(P(("dp", "mem"), None), P(("dp", "mem"), None), P(None, "mem")),
        check_vma=False,
    )
```
